32 devices in a mesh: groups: 2 (over y), src: 16 (over z, x, core).
Axes of the slice: x: 2, y: 2, z: 4, core: 2. Of those that a mesh axis runs over, the one named last changes fastest.
Arguments:
- src_points: bfloat16 [256, 64, 256], P(('groups', 'src')), parts along dimension 0, may hold values from -1.5 to 1.5
- tgt_points: bfloat16 [256, 64, 256], P(('groups', 'src')), parts along dimension 0, may hold values from -1.5 to 1.5
- g_init: float32 [256, 256], P(('groups', 'src')), parts along dimension 0, may hold values from 2 to 66
- far_src: float32 [256, 256], P(('groups', 'src')), parts along dimension 0, may hold values from 10 to 22
- far_tgt: float32 [256, 256], P(('groups', 'src')), parts along dimension 0, may hold values from -160 to -14
- cand_owner: int32 [256, 8], P(('groups', 'src')), parts along dimension 0, may hold values from 0 to 15, all different within a row; in each aligned block of 8 rows (0 to 7, 8 to 15, ...) at most 4 rows name the same one
- cand_local: int32 [256, 8], P(('groups', 'src')), parts along dimension 0, may hold values from 0 to 7
Outputs:
- src_potential: float32 [256, 256], P(('groups', 'src')), parts along dimension 0
- tgt_potential: float32 [256, 256], P(('groups', 'src')), parts along dimension 0
The draws below stay inside these ranges and needn't reach their ends.
There are 2 independent parts, one for each index of `groups`. The reference program is written for one: setup_inputs(seed, part) draws one part's arguments, and reference() takes and returns one part's arrays. A program takes and returns all parts, laid end to end along the dimension named above; each array names one. Nothing has to cross between parts.
Inputs may be any that keep to these rules, and one draw needn't show every extreme that they name: `cand_owner`: each source cluster names 8 different shards; among the 8 source clusters of one device at most 4 name the same shard, and in every draw some device names some shard exactly 4 times.
All inputs are finite; a program needn't handle non-finite values.
Results may differ from the reference program's by a relative error of at most 0.0003.
Values may be sent and summed in bfloat16 or wider, within the bound.
A program may use at most 64 MiB of HBM per device.

```python
import math
import jax
import jax.numpy as jnp
import numpy as np
from jax import lax

D = 64
PTS = 256
K = 8
ITERS = 2
SC_DEV = 8
TC_DEV = 8
CAP = 4
SC = 128
TC = 128
N_SRC = 16


def draw_g_init(key, part):
    base = jax.random.uniform(jax.random.fold_in(key, 1), (TC, PTS), jnp.float32, 2.0, 6.0)
    return base


def draw_far_tgt(key, part):
    base = jax.random.uniform(jax.random.fold_in(key, 3), (TC, PTS), jnp.float32, -26.0, -14.0)
    return base


def set_ends(result, stream_key, least, top_value):
    shape = result.shape
    place = [jax.random.randint(jax.random.fold_in(stream_key, axis), (), 0, shape[axis]) for axis in range(len(shape))]
    result = result.at[tuple(place)].set(least)
    longest = shape.index(max(shape))
    place[longest] = (place[longest] + 1) % shape[longest]
    return result.at[tuple(place)].set(top_value)


def steps_of(own_key, shape, split, low, largest):
    loudness = 1.0
    for position, blocks in split:
        steps = jax.random.uniform(jax.random.fold_in(jax.random.fold_in(own_key, 6), position), (blocks,), jnp.float32, low / len(split), largest / len(split))
        loudness = loudness * jnp.repeat(jnp.exp(steps), shape[position] // blocks).reshape((-1,) + (1,) * (len(shape) - 1 - position))
    return loudness


def shared_out(own_key, own, number, rows, number_of, top, limit, skew):
    order = jax.random.permutation(own_key, number_of)
    crowded, ordinary = load_shares(number_of, rows * top, limit, skew, True), load_shares(number_of, rows * top, limit, skew, False)
    places = jnp.arange(number_of)

    def named(sizes, rotation):
        used = int((sizes > 0).sum())
        fixed = max(1, used // 4)
        shifted = fixed + (places - fixed + rotation * (used - fixed)) % max(1, number_of - fixed)
        return jnp.zeros((number_of,), jnp.int32).at[order[jnp.where(places < fixed, places, shifted)]].set(jnp.asarray(sizes, jnp.int32))

    sizes = jnp.where(number % 4 == 0, named(crowded, number // 4), named(ordinary, number - number // 4 - 1))
    mixed = jax.random.permutation(jax.random.fold_in(own, 3), number_of)
    donor, taker = mixed[0:number_of // 2 * 2:2], mixed[1:number_of // 2 * 2:2]
    margin = jnp.minimum(sizes[donor] - 1, limit - sizes[taker]) // 2
    margin = jnp.where((donor == order[0]) | (taker == order[0]) | (sizes[taker] == 0), 0, jnp.maximum(margin, 0))
    shifted = jax.random.randint(jax.random.fold_in(own, 4), (number_of // 2,), 0, 1 << 20) % (margin + 1)
    sizes = sizes.at[donor].add(-shifted).at[taker].add(shifted)
    members = jnp.searchsorted(jnp.cumsum(sizes), jnp.arange(rows * top), side="right").astype(jnp.int32)
    table = members.reshape(top, rows).T
    table = table[jax.random.permutation(jax.random.fold_in(own, 1), rows)]
    rotation = jax.random.randint(jax.random.fold_in(own, 2), (rows, 1), 0, top)
    return jnp.take_along_axis(table, (jnp.arange(top)[None, :] + rotation) % top, axis=1)


def load_shares(amount, total, reach, lean, full):
    portions = [(1 << 20) // math.isqrt(standing ** lean) + 1 for standing in range(1, amount + 1)]
    largest = reach if full else min(reach, max(-(-total // amount), total * portions[0] // sum(portions)))
    least = 1 if total - largest >= amount - 1 else 0
    counts, surplus = [largest] + [least] * (amount - 1), total - largest - least * (amount - 1)
    while surplus > 0:
        free = [i for i in range(1, amount) if counts[i] < largest] or [i for i in range(1, amount) if counts[i] < reach]
        whole, left = sum([portions[i] for i in free]), surplus
        for i in free:
            more = min(reach - counts[i], max(1, left * portions[i] // whole), surplus)
            counts[i] = counts[i] + more
            surplus = surplus - more
    return np.array(counts)


def scatter_about(own_key, extent, scale, most, cuts=(), held_as=jnp.bfloat16):
    values = jax.random.normal(own_key, extent, jnp.float32) * scale
    if len(cuts) > 0:
        values = steps_of(own_key, extent, cuts, -0.22, 0.18) * values
    return jnp.clip(values, min=-most, max=most).astype(held_as)


def setup_inputs(seed: int = 0, part: int = 0) -> dict:
    keys = jax.random.split(jax.random.key(seed), 8)
    own_keys = jax.random.split(jax.random.fold_in(keys[7], part), 8)
    src_points = scatter_about(own_keys[0], (SC, D, PTS), 0.25, 1.5, ((0, 16),))
    tgt_points = scatter_about(own_keys[1], (TC, D, PTS), 0.25, 1.5, ((0, 16),))
    g_init = draw_g_init(jax.random.fold_in(jax.random.fold_in(keys[7], part), 71), part)
    far_src = jnp.clip(10.0 + 12.0 * jax.random.uniform(own_keys[3], (SC, PTS), jnp.float32) ** steps_of(own_keys[3], (SC, PTS), ((0, 16),), -0.2, 0.2), 10.0, 22.0)
    far_tgt = draw_far_tgt(jax.random.fold_in(jax.random.fold_in(keys[7], part), 71), part)
    cand_owner_keys = jax.random.split(jax.random.fold_in(own_keys[5], 1), SC // SC_DEV)
    cand_owner_turns = jax.random.permutation(jax.random.fold_in(own_keys[5], 3), SC // SC_DEV)
    cand_owner = jax.vmap(lambda own, number: shared_out(jax.random.fold_in(own_keys[5], 2), own, number, SC_DEV, N_SRC, K, CAP, 2))(cand_owner_keys, cand_owner_turns).reshape((SC, K))
    cand_local = set_ends(jax.random.randint(own_keys[6], (SC, K), 0, TC_DEV), jax.random.fold_in(own_keys[6], 1), 0, TC_DEV - 1).astype(jnp.int32)
    return {"src_points": src_points, "tgt_points": tgt_points, "g_init": g_init, "far_src": far_src, "far_tgt": far_tgt, "cand_owner": cand_owner, "cand_local": cand_local}


SCALE_EPS = 0.25
KEEP_TAU = 0.8


def half_norms(blocks):
    wide = blocks.astype(jnp.float32)
    return 0.5 * jnp.sum(wide * wide, axis=-2)


def reference(src_points, tgt_points, g_init, far_src, far_tgt, cand_owner, cand_local):
    cand = (cand_owner * TC_DEV + cand_local).astype(jnp.int32)
    src_half = half_norms(src_points)
    tgt_half = half_norms(tgt_points)
    indices = jnp.arange(SC, dtype=jnp.int32)

    def tile_cost(index):
        targets = cand[index]
        src_block = src_points[index].astype(jnp.float32)
        tgt_block = tgt_points[targets].astype(jnp.float32)
        inner = jnp.einsum("dp,kdq->pkq", src_block, tgt_block, precision=lax.Precision.HIGHEST)
        cost = src_half[index][:, None, None] + tgt_half[targets][None, :, :] - inner
        return cost, targets

    tgt_pot = g_init
    src_pot = jnp.zeros((SC, PTS), jnp.float32)
    for iteration in range(ITERS):
        def row_update(index):
            cost, targets = tile_cost(index)
            scores = (tgt_pot[targets][None, :, :] - cost) / SCALE_EPS
            far_term = far_src[index]
            highest = jnp.maximum(jnp.max(scores, axis=(1, 2)), far_term)
            total = jnp.exp(far_term - highest) + jnp.sum(jnp.exp(scores - highest[:, None, None]), axis=(1, 2))
            return -KEEP_TAU * SCALE_EPS * (highest + jnp.log(total))

        src_pot = lax.map(row_update, indices)

        def column_update(index):
            cost, targets = tile_cost(index)
            scores = (src_pot[index][:, None, None] - cost) / SCALE_EPS
            highest = jnp.max(scores, axis=0)
            total = jnp.sum(jnp.exp(scores - highest[None, :, :]), axis=0)
            return highest, total

        col_high, col_total = lax.map(column_update, indices)
        flat_ids = cand.reshape(SC * K)
        col_high = col_high.reshape(SC * K, PTS)
        col_total = col_total.reshape(SC * K, PTS)
        best = far_tgt.at[flat_ids].max(col_high)
        weights = col_total * jnp.exp(col_high - best[flat_ids])
        summed = jnp.exp(far_tgt - best).at[flat_ids].add(weights)
        tgt_pot = -KEEP_TAU * SCALE_EPS * (best + jnp.log(summed))
    return src_pot, tgt_pot
```

```python
import functools
import math

import jax
import jax.numpy as jnp
from jax import lax
from jax.experimental import pallas as pl
from jax.experimental.pallas import tpu as pltpu
from jax.sharding import PartitionSpec as P

ITERS = 2
SCALE_EPS = 0.25
KEEP_TAU = 0.8
VERY_LOW = -1e30
LOG2E = math.log2(math.e)
C = LOG2E / SCALE_EPS
OUT = -KEEP_TAU * SCALE_EPS / LOG2E
ROWS = 32
MESH = pl.DeviceIdType.MESH


def kernel(
    shards,
    x_ref, y_ref, g0_ref, far_src_ref, far_tgt_ref, owner_ref, local_ref,
    u_ref, v_ref,
    gathered, tiles, xt, far_col, norm_col, a_bc, u_acc, col_lse, b_own, b_all, send_blk, recv_blk,
    which_k, which_local,
    fwd_send, fwd_recv, bwd_send, bwd_recv, sib_send, sib_recv, small_send, small_recv,
):
    src_count, depth, points = x_ref.shape
    tgt_count = y_ref.shape[0]
    per_cluster = owner_ref.shape[1]
    half = tgt_count // 2
    group = lax.axis_index("groups")
    me = lax.axis_index("src")
    core = lax.rem(me, 2)
    chip = me // 2
    chips = shards // 2
    units = chips - 1
    place = jnp.where(lax.rem(chip, 2) == 0, chip // 2, chips - 1 - chip // 2)

    def shard_at(position):
        position = lax.rem(position + chips, chips)
        up = position < chips // 2
        return jnp.where(up, 2 * position, 2 * (chips - 1 - position) + 1) * 2 + core

    right = shard_at(place + 1)
    left = shard_at(place - 1)
    sibling = me + 1 - 2 * core

    barrier = pltpu.get_barrier_semaphore()

    @pl.loop(1, shards)
    def _(d):
        pl.semaphore_signal(
            barrier, inc=1, device_id=(group, lax.rem(me + d, shards)), device_id_type=MESH
        )

    wide = y_ref[...].astype(jnp.float32)
    tgt_norm = (0.5 * C) * jnp.sum(wide * wide, axis=1)
    b_own[0] = C * g0_ref[...] - tgt_norm
    b_all[0, me] = b_own[0]
    gathered[me] = y_ref[...]

    pl.semaphore_wait(barrier, shards - 1)

    def ring_copy(u, forward):
        step = u // 2
        parity = lax.rem(u, 2)
        part = parity if forward else 1 - parity
        owner = shard_at(place - step if forward else place + step)
        piece = gathered.at[owner, pl.ds(part * half, half)]
        sends, recvs = (fwd_send, fwd_recv) if forward else (bwd_send, bwd_recv)
        return pltpu.make_async_remote_copy(
            src_ref=piece, dst_ref=piece, send_sem=sends.at[u], recv_sem=recvs.at[u],
            device_id=(group, right if forward else left), device_id_type=MESH,
        )

    def sibling_copy(u, forward):
        step = u // 2 + 1
        parity = lax.rem(u, 2)
        part = parity if forward else 1 - parity
        owner = shard_at(place - step if forward else place + step)
        piece = gathered.at[owner, pl.ds(part * half, half)]
        slot = 1 + u if forward else 1 + units + u
        return pltpu.make_async_remote_copy(
            src_ref=piece, dst_ref=piece, send_sem=sib_send.at[slot], recv_sem=sib_recv.at[slot],
            device_id=(group, sibling), device_id_type=MESH,
        )

    def own_to_sibling():
        piece = gathered.at[me]
        return pltpu.make_async_remote_copy(
            src_ref=piece, dst_ref=piece, send_sem=sib_send.at[0], recv_sem=sib_recv.at[0],
            device_id=(group, sibling), device_id_type=MESH,
        )

    def small_copy(phase, d, src, dst):
        return pltpu.make_async_remote_copy(
            src_ref=src, dst_ref=dst,
            send_sem=small_send.at[phase, d], recv_sem=small_recv.at[phase, d],
            device_id=(group, lax.rem(me + d, shards)), device_id_type=MESH,
        )

    def spread_b(i, d):
        return small_copy(2 * i, d, b_own.at[i], b_all.at[i, me])

    def return_block(i, d):
        return small_copy(
            2 * i + 1, d, send_blk.at[i, lax.rem(me + d, shards)], recv_blk.at[i, me]
        )

    def for_peers(action):
        @pl.loop(1, shards)
        def _(d):
            action(d)

    first = min(2, units)
    for u in range(first):
        ring_copy(u, True).start()
        ring_copy(u, False).start()
    own_to_sibling().start()
    for_peers(lambda d: spread_b(0, d).start())

    @pl.loop(0, src_count)
    def _(s):
        xt[s] = x_ref[s].astype(jnp.float32).T.astype(jnp.bfloat16)

    wide = x_ref[...].astype(jnp.float32)
    src_norm = (0.5 * C) * jnp.sum(wide * wide, axis=1)
    norm_turned = src_norm.T
    far_turned = (LOG2E * far_src_ref[...] + src_norm).T
    for s in range(src_count):
        norm_col[s] = norm_turned[:, s : s + 1]
        far_col[s] = far_turned[:, s : s + 1]

    @pl.loop(0, src_count)
    def _(s):
        owners = [owner_ref[s, k] for k in range(per_cluster)]
        locals_ = [local_ref[s, k] for k in range(per_cluster)]

        @pl.loop(0, shards)
        def _(d):
            kk = jnp.int32(0)
            ll = jnp.int32(-1)
            for k in range(per_cluster):
                hit = owners[k] == d
                kk = jnp.where(hit, k, kk)
                ll = jnp.where(hit, locals_[k], ll)
            which_k[d, s] = kk
            which_local[d, s] = ll

    @pl.loop(first, units)
    def _(u):
        for forward in (True, False):
            ring_copy(u - 2, forward).wait_recv()
            ring_copy(u, forward).start()
            sibling_copy(u - 2, forward).start()

    for u in range(max(0, units - 2), units):
        for forward in (True, False):
            ring_copy(u, forward).wait_recv()
            sibling_copy(u, forward).start()

    own_to_sibling().wait()

    @pl.loop(0, units)
    def _(u):
        for forward in (True, False):
            ring_copy(u, forward).wait_send()
            sibling_copy(u, forward).wait()

    for_peers(lambda d: spread_b(0, d).wait())

    rows8 = lax.broadcasted_iota(jnp.int32, (tgt_count, points), 0)
    lanes = lax.broadcasted_iota(jnp.int32, (points, 128), 1)
    u_acc[...] = jnp.zeros_like(u_acc)
    far_tgt = LOG2E * far_tgt_ref[...] + tgt_norm

    for i in range(ITERS):

        @pl.loop(0, src_count)
        def _(s):
            if i == 0:
                for k in range(per_cluster):
                    tiles[s * per_cluster + k] = C * jnp.dot(
                        xt[s],
                        gathered[owner_ref[s, k], local_ref[s, k]],
                        preferred_element_type=jnp.float32,
                    )
            bias = [
                b_all[i, owner_ref[s, k], pl.ds(local_ref[s, k], 1), :] for k in range(per_cluster)
            ]
            for r in range(0, points, ROWS):
                here = pl.ds(r, ROWS)
                scores = [
                    tiles[s * per_cluster + k, here, :] + bias[k] for k in range(per_cluster)
                ]
                far = far_col[s, here, :]
                high = functools.reduce(jnp.maximum, scores)
                high = jnp.maximum(jnp.max(high, axis=1, keepdims=True), far)
                total = functools.reduce(jnp.add, [jnp.exp2(t - high) for t in scores])
                total = jnp.sum(total, axis=1, keepdims=True) + jnp.exp2(far - high)
                norm = norm_col[s, here, :]
                lse = high + jnp.log2(total) - norm
                a_bc[here, :] = jnp.broadcast_to(-KEEP_TAU * lse - norm, (ROWS, 128))
                if i == ITERS - 1:
                    u_acc[here, :] = jnp.where(lanes[:ROWS] == s, OUT * lse, u_acc[here, :])
            for k in range(per_cluster):
                for c in range(0, points, 128):
                    there = pl.ds(c, 128)
                    t = tiles[s * per_cluster + k, :, there] + a_bc[...]
                    high = jnp.max(t, axis=0, keepdims=True)
                    total = jnp.sum(jnp.exp2(t - high), axis=0, keepdims=True)
                    col_lse[s * per_cluster + k, :, there] = high + jnp.log2(total)

        @pl.loop(0, shards)
        def _(d):
            masks = [rows8 == which_local[d, s] for s in range(src_count)]
            rows = [
                jnp.where(masks[s], col_lse[s * per_cluster + which_k[d, s]], VERY_LOW)
                for s in range(src_count)
            ]
            high = functools.reduce(jnp.maximum, rows)
            total = functools.reduce(
                jnp.add,
                [jnp.where(masks[s], jnp.exp2(rows[s] - high), 0.0) for s in range(src_count)],
            )
            send_blk[i, d] = high + jnp.log2(jnp.maximum(total, 1.0))

        recv_blk[i, me] = send_blk[i, me]
        for_peers(lambda d: return_block(i, d).start())
        for_peers(lambda d: return_block(i, d).wait())
        best = lax.fori_loop(0, shards, lambda d, m: jnp.maximum(m, recv_blk[i, d]), far_tgt)
        total = lax.fori_loop(
            0, shards, lambda d, t: t + jnp.exp2(recv_blk[i, d] - best), jnp.exp2(far_tgt - best)
        )
        lse = best + jnp.log2(total) - tgt_norm
        if i == ITERS - 1:
            v_ref[...] = OUT * lse
        else:
            b_own[i + 1] = -KEEP_TAU * lse - tgt_norm
            b_all[i + 1, me] = b_own[i + 1]
            for_peers(lambda d: spread_b(i + 1, d).start())
            for_peers(lambda d: spread_b(i + 1, d).wait())

    u_ref[...] = u_acc[...].T[:src_count, :]


def per_device(src_points, tgt_points, g_init, far_src, far_tgt, cand_owner, cand_local):
    src_count, depth, points = src_points.shape
    tgt_count = tgt_points.shape[0]
    pairs = src_count * cand_owner.shape[1]
    shards = lax.axis_size("src")
    units = shards // 2 - 1
    f32 = jnp.float32
    scratch = [
        pltpu.VMEM((shards, tgt_count, depth, points), jnp.bfloat16),
        pltpu.VMEM((pairs, points, points), f32),
        pltpu.VMEM((src_count, points, depth), jnp.bfloat16),
        pltpu.VMEM((src_count, points, 1), f32),
        pltpu.VMEM((src_count, points, 1), f32),
        pltpu.VMEM((points, 128), f32),
        pltpu.VMEM((points, 128), f32),
        pltpu.VMEM((pairs, 1, points), f32),
        pltpu.VMEM((ITERS, tgt_count, points), f32),
        pltpu.VMEM((ITERS, shards, tgt_count, points), f32),
        pltpu.VMEM((ITERS, shards, tgt_count, points), f32),
        pltpu.VMEM((ITERS, shards, tgt_count, points), f32),
        pltpu.SMEM((shards, src_count), jnp.int32),
        pltpu.SMEM((shards, src_count), jnp.int32),
    ]
    sems = [units] * 4 + [1 + 2 * units] * 2
    scratch += [pltpu.SemaphoreType.DMA((n,)) for n in sems]
    scratch += [pltpu.SemaphoreType.DMA((2 * ITERS, shards))] * 2
    used = shards * tgt_count * points * (2 * depth + 4 * 3 * ITERS) + 4 * pairs * points * points
    vmem = pl.BlockSpec(memory_space=pltpu.VMEM)
    smem = pl.BlockSpec(memory_space=pltpu.SMEM)
    return pl.pallas_call(
        functools.partial(kernel, shards),
        out_shape=(
            jax.ShapeDtypeStruct((src_count, points), f32),
            jax.ShapeDtypeStruct((tgt_count, points), f32),
        ),
        in_specs=[vmem] * 5 + [smem] * 2,
        out_specs=(vmem, vmem),
        scratch_shapes=scratch,
        compiler_params=pltpu.CompilerParams(
            collective_id=0, has_side_effects=True, vmem_limit_bytes=used + (7 << 20)
        ),
    )(src_points, tgt_points, g_init, far_src, far_tgt, cand_owner, cand_local)


def solution(mesh):
    return jax.shard_map(
        per_device,
        mesh=mesh,
        in_specs=(
            P(("groups", "src"), None, None),
            P(("groups", "src"), None, None),
            P(("groups", "src"), None),
            P(("groups", "src"), None),
            P(("groups", "src"), None),
            P(("groups", "src"), None),
            P(("groups", "src"), None),
        ),
        out_specs=(P(("groups", "src"), None), P(("groups", "src"), None)),
        check_vma=False,
    )
```

```python
import functools
import math

import jax
import jax.numpy as jnp
from jax import lax
from jax.experimental import pallas as pl
from jax.experimental.pallas import tpu as pltpu
from jax.sharding import PartitionSpec as P

ITERS = 2
SCALE_EPS = 0.25
KEEP_TAU = 0.8
VERY_LOW = -1e30
LOG2E = math.log2(math.e)
C = LOG2E / SCALE_EPS
OUT = -KEEP_TAU * SCALE_EPS / LOG2E
ROWS = 32
VMEM_BYTES = 64 << 20
MESH = pl.DeviceIdType.MESH


def kernel(
    shards, capacity, early,
    x_hbm, y_hbm, g0_hbm, far_src_hbm, far_tgt_hbm, owner_hbm, local_hbm,
    u_ref, v_ref,
    x_ref, g0_ref, far_src_ref, far_tgt_ref, owner_ref, local_ref, load_sem,
    gathered, tiles, xt, far_col, norm_col, a_bc, u_acc, col_lse, b_own, b_all, send_blk, recv_blk,
    which_k, which_local, slot_at, slot_src, slot_local, part_high, part_total, stage,
    fwd_send, fwd_recv, bwd_send, bwd_recv, sib_send, sib_recv, small_send, small_recv,
):
    src_count, depth, points = x_ref.shape
    tgt_count = g0_ref.shape[0]
    per_cluster = owner_ref.shape[1]
    half = tgt_count // 2
    group = lax.axis_index("groups")
    me = lax.axis_index("src")
    core = lax.rem(me, 2)
    chip = me // 2
    chips = shards // 2
    units = chips - 1
    place = jnp.where(lax.rem(chip, 2) == 0, chip // 2, chips - 1 - chip // 2)

    def shard_at(position):
        position = lax.rem(position + chips, chips)
        up = position < chips // 2
        return jnp.where(up, 2 * position, 2 * (chips - 1 - position) + 1) * 2 + core

    right = shard_at(place + 1)
    left = shard_at(place - 1)
    sibling = me + 1 - 2 * core

    barrier = pltpu.get_barrier_semaphore()

    @pl.loop(1, shards)
    def _(d):
        pl.semaphore_signal(
            barrier, inc=1, device_id=(group, lax.rem(me + d, shards)), device_id_type=MESH
        )

    loads = [
        pltpu.make_async_copy(src, dst, load_sem.at[n])
        for n, (src, dst) in enumerate((
            (y_hbm, gathered.at[me]),
            (g0_hbm, g0_ref),
            (x_hbm, x_ref),
            (owner_hbm, owner_ref),
            (local_hbm, local_ref),
            (far_src_hbm, far_src_ref),
            (far_tgt_hbm, far_tgt_ref),
        ))
    ]
    for load in loads:
        load.start()
    loads[0].wait()
    pl.semaphore_wait(barrier, shards - 1)

    def ring_copy(u, forward):
        step = u // 2
        parity = lax.rem(u, 2)
        part = parity if forward else 1 - parity
        owner = shard_at(place - step if forward else place + step)
        piece = gathered.at[owner, pl.ds(part * half, half)]
        sends, recvs = (fwd_send, fwd_recv) if forward else (bwd_send, bwd_recv)
        return pltpu.make_async_remote_copy(
            src_ref=piece, dst_ref=piece, send_sem=sends.at[u], recv_sem=recvs.at[u],
            device_id=(group, right if forward else left), device_id_type=MESH,
        )

    def sibling_copy(u, forward):
        step = u // 2 + 1
        parity = lax.rem(u, 2)
        part = parity if forward else 1 - parity
        owner = shard_at(place - step if forward else place + step)
        piece = gathered.at[owner, pl.ds(part * half, half)]
        slot = 1 + u if forward else 1 + units + u
        return pltpu.make_async_remote_copy(
            src_ref=piece, dst_ref=piece, send_sem=sib_send.at[slot], recv_sem=sib_recv.at[slot],
            device_id=(group, sibling), device_id_type=MESH,
        )

    def own_to_sibling():
        piece = gathered.at[me]
        return pltpu.make_async_remote_copy(
            src_ref=piece, dst_ref=piece, send_sem=sib_send.at[0], recv_sem=sib_recv.at[0],
            device_id=(group, sibling), device_id_type=MESH,
        )

    def small_copy(phase, peer, src, dst):
        return pltpu.make_async_remote_copy(
            src_ref=src, dst_ref=dst,
            send_sem=small_send.at[phase], recv_sem=small_recv.at[phase],
            device_id=(group, peer), device_id_type=MESH,
        )

    def spread_b(i):
        @pl.loop(1, shards)
        def _(d):
            small_copy(2 * i, lax.rem(me + d, shards), b_own.at[i], b_all.at[i, me]).start()

    def await_all(sem, buffer):
        blocks = buffer.at[pl.ds(0, shards - 1)]
        pltpu.make_async_copy(blocks, blocks, sem).wait()

    first = min(2, units)
    for u in range(first):
        ring_copy(u, True).start()
        ring_copy(u, False).start()
    own_to_sibling().start()
    loads[1].wait()
    wide = gathered[me].astype(jnp.float32)
    tgt_norm = (0.5 * C) * jnp.sum(wide * wide, axis=1)
    b_own[0] = C * g0_ref[...] - tgt_norm
    b_all[0, me] = b_own[0]
    spread_b(0)
    for load in loads[2:]:
        load.wait()

    @pl.loop(0, src_count)
    def _(s):
        xt[s] = x_ref[s].astype(jnp.float32).T.astype(jnp.bfloat16)

    wide = x_ref[...].astype(jnp.float32)
    src_norm = (0.5 * C) * jnp.sum(wide * wide, axis=1)
    norm_turned = src_norm.T
    far_turned = (LOG2E * far_src_ref[...] + src_norm).T
    for s in range(src_count):
        norm_col[s] = norm_turned[:, s : s + 1]
        far_col[s] = far_turned[:, s : s + 1]

    @pl.loop(0, src_count)
    def _(s):
        owners = [owner_ref[s, k] for k in range(per_cluster)]
        locals_ = [local_ref[s, k] for k in range(per_cluster)]

        @pl.loop(0, shards)
        def _(d):
            kk = jnp.int32(0)
            ll = jnp.int32(-1)
            for k in range(per_cluster):
                hit = owners[k] == d
                kk = jnp.where(hit, k, kk)
                ll = jnp.where(hit, locals_[k], ll)
            which_k[d, s] = kk
            which_local[d, s] = ll

    @pl.loop(0, shards if early else 0)
    def _(d):
        count = jnp.int32(0)
        sources = [jnp.int32(0)] * capacity
        locals_ = [jnp.int32(0)] * capacity
        for s in range(src_count):
            ll = which_local[d, s]
            slot_at[d, s] = d * capacity + jnp.minimum(count, capacity - 1)
            for c in range(capacity):
                take = (ll >= 0) & (count == c)
                sources[c] = jnp.where(take, s, sources[c])
                locals_[c] = jnp.where(take, ll, locals_[c])
            count = count + jnp.where(ll >= 0, 1, 0)
        for c in range(capacity):
            slot_src[d, c] = sources[c]
            slot_local[d, c] = locals_[c]

    def row_parts(d):
        if early:
            stage[...] = gathered[d]

            @pl.loop(0, capacity)
            def _(c):
                slot = d * capacity + c
                local = slot_local[d, c]
                bias = b_all[0, d, pl.ds(local, 1), :]
                t = C * jnp.dot(
                    xt[slot_src[d, c]], stage[local], preferred_element_type=jnp.float32
                )
                tiles[slot] = t
                t = t + bias
                lanes_of = [t[:, c : c + 128] for c in range(0, points, 128)]
                high = functools.reduce(jnp.maximum, lanes_of)
                part_high[slot] = high
                part_total[slot] = functools.reduce(
                    jnp.add, [jnp.exp2(p - high) for p in lanes_of]
                )

    def across(owner):
        return owner + 1 - 2 * core

    steps = (units - 1) // 2

    @pl.loop(0, steps)
    def _(t):
        for h in range(2):
            u = 2 * t + h
            for forward in (True, False):
                ring_copy(u, forward).wait_recv()

                @pl.when(u + 2 < units)
                def _():
                    ring_copy(u + 2, forward).start()

                sibling_copy(u, forward).start()

        @pl.when(t == 0)
        def _():
            await_all(small_recv.at[0], b_all.at[0])
            own_to_sibling().wait_recv()
            row_parts(me)
            row_parts(sibling)

        @pl.when(t > 0)
        def _():
            for forward in (True, False):
                for h in range(2):
                    sibling_copy(2 * t - 2 + h, forward).wait_recv()
                row_parts(across(shard_at(place - t if forward else place + t)))

        row_parts(shard_at(place - t - 1))
        row_parts(shard_at(place + t + 1))

    last = units - 1
    for forward in (True, False):
        ring_copy(last, forward).wait_recv()
        sibling_copy(last, forward).start()
    for forward in (True, False):
        for h in range(2):
            sibling_copy(2 * steps - 2 + h, forward).wait_recv()
        row_parts(across(shard_at(place - steps if forward else place + steps)))
    row_parts(shard_at(place + steps + 1))
    for forward in (True, False):
        sibling_copy(last, forward).wait_recv()
    row_parts(across(shard_at(place + steps + 1)))

    rows8 = lax.broadcasted_iota(jnp.int32, (tgt_count, points), 0)
    lanes = lax.broadcasted_iota(jnp.int32, (points, 128), 1)
    u_acc[...] = jnp.zeros_like(u_acc)
    far_tgt = LOG2E * far_tgt_ref[...] + tgt_norm

    for i in range(ITERS):

        @pl.loop(0, src_count)
        def _(s):
            if early:
                at = [slot_at[owner_ref[s, k], s] for k in range(per_cluster)]
            else:
                at = [s * per_cluster + k for k in range(per_cluster)]
            if i == 0 and not early:
                for k in range(per_cluster):
                    tiles[at[k]] = C * jnp.dot(
                        xt[s],
                        gathered[owner_ref[s, k], local_ref[s, k]],
                        preferred_element_type=jnp.float32,
                    )
            bias = [
                b_all[i, owner_ref[s, k], pl.ds(local_ref[s, k], 1), :] for k in range(per_cluster)
            ]
            for r in range(0, points, ROWS):
                here = pl.ds(r, ROWS)
                far = far_col[s, here, :]
                if i == 0 and early:
                    highs = [part_high[at[k], here, :] for k in range(per_cluster)]
                    high = functools.reduce(jnp.maximum, highs)
                    high = jnp.maximum(jnp.max(high, axis=1, keepdims=True), far)
                    total = functools.reduce(
                        jnp.add,
                        [
                            part_total[at[k], here, :] * jnp.exp2(highs[k] - high)
                            for k in range(per_cluster)
                        ],
                    )
                else:
                    scores = [tiles[at[k], here, :] + bias[k] for k in range(per_cluster)]
                    high = functools.reduce(jnp.maximum, scores)
                    high = jnp.maximum(jnp.max(high, axis=1, keepdims=True), far)
                    total = functools.reduce(jnp.add, [jnp.exp2(t - high) for t in scores])
                total = jnp.sum(total, axis=1, keepdims=True) + jnp.exp2(far - high)
                norm = norm_col[s, here, :]
                lse = high + jnp.log2(total) - norm
                a_bc[here, :] = jnp.broadcast_to(-KEEP_TAU * lse - norm, (ROWS, 128))
                if i == ITERS - 1:
                    u_acc[here, :] = jnp.where(lanes[:ROWS] == s, OUT * lse, u_acc[here, :])
            for k in range(per_cluster):
                for c in range(0, points, 128):
                    there = pl.ds(c, 128)
                    t = tiles[at[k], :, there] + a_bc[...]
                    high = jnp.max(t, axis=0, keepdims=True)
                    total = jnp.sum(jnp.exp2(t - high), axis=0, keepdims=True)
                    col_lse[s * per_cluster + k, :, there] = high + jnp.log2(total)

        @pl.loop(0, shards)
        def _(d):
            masks = [rows8 == which_local[d, s] for s in range(src_count)]
            rows = [
                jnp.where(masks[s], col_lse[s * per_cluster + which_k[d, s]], VERY_LOW)
                for s in range(src_count)
            ]
            high = functools.reduce(jnp.maximum, rows)
            total = functools.reduce(
                jnp.add,
                [jnp.where(masks[s], jnp.exp2(rows[s] - high), 0.0) for s in range(src_count)],
            )
            send_blk[i, d] = high + jnp.log2(jnp.maximum(total, 1.0))

        @pl.loop(1, shards)
        def _(d):
            peer = lax.rem(me + d, shards)
            small_copy(2 * i + 1, peer, send_blk.at[i, peer], recv_blk.at[i, me]).start()

        recv_blk[i, me] = send_blk[i, me]
        await_all(small_recv.at[2 * i + 1], recv_blk.at[i])
        best = lax.fori_loop(0, shards, lambda d, m: jnp.maximum(m, recv_blk[i, d]), far_tgt)
        total = lax.fori_loop(
            0, shards, lambda d, t: t + jnp.exp2(recv_blk[i, d] - best), jnp.exp2(far_tgt - best)
        )
        lse = best + jnp.log2(total) - tgt_norm
        if i == ITERS - 1:
            v_ref[...] = OUT * lse
        else:
            b_own[i + 1] = -KEEP_TAU * lse - tgt_norm
            b_all[i + 1, me] = b_own[i + 1]
            spread_b(i + 1)
            await_all(small_recv.at[2 * i + 2], b_all.at[i + 1])

    u_ref[...] = u_acc[...].T[:src_count, :]

    own_to_sibling().wait_send()

    @pl.loop(0, units)
    def _(u):
        for forward in (True, False):
            ring_copy(u, forward).wait_send()
            sibling_copy(u, forward).wait_send()

    for phase in range(2 * ITERS):
        await_all(small_send.at[phase], recv_blk.at[0])


def per_device(src_points, tgt_points, g_init, far_src, far_tgt, cand_owner, cand_local):
    src_count, depth, points = src_points.shape
    tgt_count = tgt_points.shape[0]
    pairs = src_count * cand_owner.shape[1]
    shards = lax.axis_size("src")
    units = shards // 2 - 1
    capacity = max(2, min(src_count // 2, 2 * pairs // shards))
    early = shards * capacity <= pairs and units >= 3
    parts = pairs if early else 1
    f32 = jnp.float32
    scratch = [
        pltpu.VMEM(src_points.shape, jnp.bfloat16),
        pltpu.VMEM(g_init.shape, f32),
        pltpu.VMEM(far_src.shape, f32),
        pltpu.VMEM(far_tgt.shape, f32),
        pltpu.SMEM(cand_owner.shape, jnp.int32),
        pltpu.SMEM(cand_local.shape, jnp.int32),
        pltpu.SemaphoreType.DMA((7,)),
        pltpu.VMEM((shards, tgt_count, depth, points), jnp.bfloat16),
        pltpu.VMEM((pairs, points, points), f32),
        pltpu.VMEM((src_count, points, depth), jnp.bfloat16),
        pltpu.VMEM((src_count, points, 1), f32),
        pltpu.VMEM((src_count, points, 1), f32),
        pltpu.VMEM((points, 128), f32),
        pltpu.VMEM((points, 128), f32),
        pltpu.VMEM((pairs, 1, points), f32),
        pltpu.VMEM((ITERS, tgt_count, points), f32),
        pltpu.VMEM((ITERS, shards, tgt_count, points), f32),
        pltpu.VMEM((ITERS, shards, tgt_count, points), f32),
        pltpu.VMEM((ITERS, shards, tgt_count, points), f32),
        pltpu.SMEM((shards, src_count), jnp.int32),
        pltpu.SMEM((shards, src_count), jnp.int32),
    ]
    scratch += [pltpu.SMEM((shards, n), jnp.int32) for n in (src_count, capacity, capacity)]
    scratch += [pltpu.VMEM((parts, points, 128), f32)] * 2
    scratch += [pltpu.VMEM(tgt_points.shape, jnp.bfloat16)]
    sems = [units] * 4 + [1 + 2 * units] * 2
    scratch += [pltpu.SemaphoreType.DMA((n,)) for n in sems]
    scratch += [pltpu.SemaphoreType.DMA((2 * ITERS,))] * 2
    vmem = pl.BlockSpec(memory_space=pltpu.VMEM)
    hbm = pl.BlockSpec(memory_space=pltpu.HBM)
    return pl.pallas_call(
        functools.partial(kernel, shards, capacity, early),
        out_shape=(
            jax.ShapeDtypeStruct((src_count, points), f32),
            jax.ShapeDtypeStruct((tgt_count, points), f32),
        ),
        in_specs=[hbm] * 7,
        out_specs=(vmem, vmem),
        scratch_shapes=scratch,
        compiler_params=pltpu.CompilerParams(
            collective_id=0, has_side_effects=True, vmem_limit_bytes=VMEM_BYTES
        ),
    )(src_points, tgt_points, g_init, far_src, far_tgt, cand_owner, cand_local)


def solution(mesh):
    return jax.shard_map(
        per_device,
        mesh=mesh,
        in_specs=(
            P(("groups", "src"), None, None),
            P(("groups", "src"), None, None),
            P(("groups", "src"), None),
            P(("groups", "src"), None),
            P(("groups", "src"), None),
            P(("groups", "src"), None),
            P(("groups", "src"), None),
        ),
        out_specs=(P(("groups", "src"), None), P(("groups", "src"), None)),
        check_vma=False,
    )
```

```python
import functools
import math

import jax
import jax.numpy as jnp
from jax import lax
from jax.experimental import pallas as pl
from jax.experimental.pallas import tpu as pltpu
from jax.sharding import PartitionSpec as P

ITERS = 2
SCALE_EPS = 0.25
KEEP_TAU = 0.8
VERY_LOW = -1e30
LOG2E = math.log2(math.e)
C = LOG2E / SCALE_EPS
OUT = -KEEP_TAU * SCALE_EPS / LOG2E
ROWS = 16
VMEM_BYTES = 64 << 20
MESH = pl.DeviceIdType.MESH


def kernel(
    shards, capacity, early,
    x_hbm, y_hbm, g0_hbm, far_src_hbm, far_tgt_hbm, owner_hbm, local_hbm,
    u_ref, v_ref,
    x_ref, g0_ref, far_src_ref, far_tgt_ref, owner_ref, local_ref, load_sem,
    gathered, tiles, xt, far_col, norm_col, a_bc, u_acc, col_lse, b_own, b_all, send_blk, recv_blk,
    which_k, which_local, slot_at, slot_src, slot_local, slot_row, row_high, row_total, part_high, part_total, stage,
    fwd_send, fwd_recv, bwd_send, bwd_recv, sib_send, sib_recv, small_send, small_recv,
):
    src_count, depth, points = x_ref.shape
    tgt_count = g0_ref.shape[0]
    per_cluster = owner_ref.shape[1]
    half = tgt_count // 2
    group = lax.axis_index("groups")
    me = lax.axis_index("src")
    core = lax.rem(me, 2)
    chip = me // 2
    chips = shards // 2
    units = chips - 1
    place = jnp.where(lax.rem(chip, 2) == 0, chip // 2, chips - 1 - chip // 2)

    def shard_at(position):
        position = lax.rem(position + chips, chips)
        up = position < chips // 2
        return jnp.where(up, 2 * position, 2 * (chips - 1 - position) + 1) * 2 + core

    right = shard_at(place + 1)
    left = shard_at(place - 1)
    sibling = me + 1 - 2 * core

    barrier = pltpu.get_barrier_semaphore()

    @pl.loop(1, shards)
    def _(d):
        pl.semaphore_signal(
            barrier, inc=1, device_id=(group, lax.rem(me + d, shards)), device_id_type=MESH
        )

    loads = [
        pltpu.make_async_copy(src, dst, load_sem.at[n])
        for n, (src, dst) in enumerate((
            (y_hbm, gathered.at[me]),
            (g0_hbm, g0_ref),
            (x_hbm, x_ref),
            (owner_hbm, owner_ref),
            (local_hbm, local_ref),
            (far_src_hbm, far_src_ref),
            (far_tgt_hbm, far_tgt_ref),
        ))
    ]
    for load in loads:
        load.start()
    loads[0].wait()
    pl.semaphore_wait(barrier, shards - 1)

    def ring_copy(u, forward):
        step = u // 2
        parity = lax.rem(u, 2)
        part = parity if forward else 1 - parity
        owner = shard_at(place - step if forward else place + step)
        piece = gathered.at[owner, pl.ds(part * half, half)]
        sends, recvs = (fwd_send, fwd_recv) if forward else (bwd_send, bwd_recv)
        return pltpu.make_async_remote_copy(
            src_ref=piece, dst_ref=piece, send_sem=sends.at[u], recv_sem=recvs.at[u],
            device_id=(group, right if forward else left), device_id_type=MESH,
        )

    def sibling_copy(u, forward):
        step = u // 2 + 1
        parity = lax.rem(u, 2)
        part = parity if forward else 1 - parity
        owner = shard_at(place - step if forward else place + step)
        piece = gathered.at[owner, pl.ds(part * half, half)]
        slot = 1 + u if forward else 1 + units + u
        return pltpu.make_async_remote_copy(
            src_ref=piece, dst_ref=piece, send_sem=sib_send.at[slot], recv_sem=sib_recv.at[slot],
            device_id=(group, sibling), device_id_type=MESH,
        )

    def own_to_sibling():
        piece = gathered.at[me]
        return pltpu.make_async_remote_copy(
            src_ref=piece, dst_ref=piece, send_sem=sib_send.at[0], recv_sem=sib_recv.at[0],
            device_id=(group, sibling), device_id_type=MESH,
        )

    def small_copy(phase, peer, src, dst):
        return pltpu.make_async_remote_copy(
            src_ref=src, dst_ref=dst,
            send_sem=small_send.at[phase], recv_sem=small_recv.at[phase],
            device_id=(group, peer), device_id_type=MESH,
        )

    def spread_b(i):
        @pl.loop(1, shards)
        def _(d):
            small_copy(2 * i, lax.rem(me + d, shards), b_own.at[i], b_all.at[i, me]).start()

    def await_all(sem, buffer):
        blocks = buffer.at[pl.ds(0, shards - 1)]
        pltpu.make_async_copy(blocks, blocks, sem).wait()

    first = min(2, units)
    for u in range(first):
        ring_copy(u, True).start()
        ring_copy(u, False).start()
    own_to_sibling().start()
    loads[1].wait()
    wide = gathered[me].astype(jnp.float32)
    tgt_norm = (0.5 * C) * jnp.sum(wide * wide, axis=1)
    b_own[0] = C * g0_ref[...] - tgt_norm
    b_all[0, me] = b_own[0]
    spread_b(0)
    for load in loads[2:]:
        load.wait()

    @pl.loop(0, src_count)
    def _(s):
        xt[s] = x_ref[s].astype(jnp.float32).T.astype(jnp.bfloat16)

    wide = x_ref[...].astype(jnp.float32)
    src_norm = (0.5 * C) * jnp.sum(wide * wide, axis=1)
    norm_turned = src_norm.T
    far_turned = (LOG2E * far_src_ref[...] + src_norm).T
    for s in range(src_count):
        norm_col[s] = jnp.broadcast_to(norm_turned[:, s : s + 1], (points, 128))
        far_col[s] = jnp.broadcast_to(far_turned[:, s : s + 1], (points, 128))

    @pl.loop(0, src_count)
    def _(s):
        owners = [owner_ref[s, k] for k in range(per_cluster)]
        locals_ = [local_ref[s, k] for k in range(per_cluster)]

        @pl.loop(0, shards)
        def _(d):
            kk = jnp.int32(0)
            ll = jnp.int32(-1)
            for k in range(per_cluster):
                hit = owners[k] == d
                kk = jnp.where(hit, k, kk)
                ll = jnp.where(hit, locals_[k], ll)
            which_k[d, s] = kk
            which_local[d, s] = ll

    @pl.loop(0, shards if early else 0)
    def _(d):
        count = jnp.int32(0)
        sources = [jnp.int32(0)] * capacity
        locals_ = [jnp.int32(-1)] * capacity
        for s in range(src_count):
            ll = which_local[d, s]
            slot_at[d, s] = d * capacity + jnp.minimum(count, capacity - 1)
            for c in range(capacity):
                take = (ll >= 0) & (count == c)
                sources[c] = jnp.where(take, s, sources[c])
                locals_[c] = jnp.where(take, ll, locals_[c])
            count = count + jnp.where(ll >= 0, 1, 0)
        for c in range(capacity):
            slot_src[d, c] = sources[c]
            slot_local[d, c] = jnp.maximum(locals_[c], 0)
            slot_row[d, c] = locals_[c]

    def row_parts(d):
        if early:
            stage[...] = gathered[d]

            @pl.loop(0, capacity)
            def _(c):
                slot = d * capacity + c
                local = slot_local[d, c]
                bias = b_all[0, d, pl.ds(local, 1), :]
                t = C * jnp.dot(
                    xt[slot_src[d, c]], stage[local], preferred_element_type=jnp.float32
                )
                tiles[slot] = t
                t = t + bias
                lanes_of = [t[:, c : c + 128] for c in range(0, points, 128)]
                high = functools.reduce(jnp.maximum, lanes_of)
                part_high[slot] = high
                part_total[slot] = functools.reduce(
                    jnp.add, [jnp.exp2(p - high) for p in lanes_of]
                )

    def across(owner):
        return owner + 1 - 2 * core

    steps = (units - 1) // 2

    @pl.loop(0, steps)
    def _(t):
        for h in range(2):
            u = 2 * t + h
            for forward in (True, False):
                ring_copy(u, forward).wait_recv()

                @pl.when(u + 2 < units)
                def _():
                    ring_copy(u + 2, forward).start()

                sibling_copy(u, forward).start()

        @pl.when(t == 0)
        def _():
            await_all(small_recv.at[0], b_all.at[0])
            own_to_sibling().wait_recv()
            row_parts(me)
            row_parts(sibling)

        @pl.when(t > 0)
        def _():
            for forward in (True, False):
                for h in range(2):
                    sibling_copy(2 * t - 2 + h, forward).wait_recv()
                row_parts(across(shard_at(place - t if forward else place + t)))

        row_parts(shard_at(place - t - 1))
        row_parts(shard_at(place + t + 1))

    last = units - 1
    for forward in (True, False):
        ring_copy(last, forward).wait_recv()
        sibling_copy(last, forward).start()
    for forward in (True, False):
        for h in range(2):
            sibling_copy(2 * steps - 2 + h, forward).wait_recv()
        row_parts(across(shard_at(place - steps if forward else place + steps)))
    row_parts(shard_at(place + steps + 1))
    for forward in (True, False):
        sibling_copy(last, forward).wait_recv()
    row_parts(across(shard_at(place + steps + 1)))

    rows8 = lax.broadcasted_iota(jnp.int32, (tgt_count, points), 0)
    lanes = lax.broadcasted_iota(jnp.int32, (points, 128), 1)
    u_acc[...] = jnp.zeros_like(u_acc)
    far_tgt = LOG2E * far_tgt_ref[...] + tgt_norm

    def column_lse(tile, s):
        pieces = []
        for c in range(0, points, 128):
            t = tile[:, pl.ds(c, 128)] + a_bc[s]
            high = jnp.max(t, axis=0, keepdims=True)
            total = jnp.sum(jnp.exp2(t - high), axis=0, keepdims=True)
            pieces.append(high + jnp.log2(total))
        return jnp.concatenate(pieces, axis=1)

    for i in range(ITERS):

        @pl.loop(0, src_count)
        def _(s):
            if early:
                at = [slot_at[owner_ref[s, k], s] for k in range(per_cluster)]
            else:
                at = [s * per_cluster + k for k in range(per_cluster)]
            if i == 0 and not early:
                for k in range(per_cluster):
                    tiles[at[k]] = C * jnp.dot(
                        xt[s],
                        gathered[owner_ref[s, k], local_ref[s, k]],
                        preferred_element_type=jnp.float32,
                    )
            bias = [
                b_all[i, owner_ref[s, k], pl.ds(local_ref[s, k], 1), :] for k in range(per_cluster)
            ]
            for r in range(0, points, ROWS):
                here = pl.ds(r, ROWS)
                if i == 0 and early:
                    highs = [part_high[at[k], here, :] for k in range(per_cluster)]
                    high = functools.reduce(jnp.maximum, highs)
                    total = functools.reduce(
                        jnp.add,
                        [
                            part_total[at[k], here, :] * jnp.exp2(highs[k] - high)
                            for k in range(per_cluster)
                        ],
                    )
                else:
                    scores = [
                        tiles[at[k], here, pl.ds(c, 128)] + bias[k][:, c : c + 128]
                        for k in range(per_cluster)
                        for c in range(0, points, 128)
                    ]
                    high = functools.reduce(jnp.maximum, scores)
                    total = functools.reduce(jnp.add, [jnp.exp2(t - high) for t in scores])
                row_high[here, :] = high
                row_total[here, :] = total
            far = far_col[s]
            norm = norm_col[s]
            high = row_high[...]
            top = jnp.maximum(
                jnp.broadcast_to(jnp.max(high, axis=1, keepdims=True), high.shape), far
            )
            total = row_total[...] * jnp.exp2(high - top)
            total = jnp.broadcast_to(jnp.sum(total, axis=1, keepdims=True), high.shape)
            lse = top + jnp.log2(total + jnp.exp2(far - top)) - norm
            a_bc[s] = -KEEP_TAU * lse - norm
            if i == ITERS - 1:
                u_acc[...] = jnp.where(lanes == s, OUT * lse, u_acc[...])
            if not early:
                for k in range(per_cluster):
                    col_lse[s * per_cluster + k] = column_lse(tiles.at[at[k]], s)

        @pl.loop(1, shards + 1)
        def _(o):
            d = lax.rem(me + o, shards)
            if early:
                masks = [rows8 == slot_row[d, c] for c in range(capacity)]
                parts = [
                    column_lse(tiles.at[d * capacity + c], slot_src[d, c]) for c in range(capacity)
                ]
            else:
                masks = [rows8 == which_local[d, s] for s in range(src_count)]
                parts = [
                    col_lse[s * per_cluster + which_k[d, s]] for s in range(src_count)
                ]
            rows = [jnp.where(m, p, VERY_LOW) for m, p in zip(masks, parts)]
            high = functools.reduce(jnp.maximum, rows)
            total = functools.reduce(
                jnp.add, [jnp.where(m, jnp.exp2(p - high), 0.0) for m, p in zip(masks, rows)]
            )
            send_blk[i, d] = high + jnp.log2(jnp.maximum(total, 1.0))

            @pl.when(o < shards)
            def _():
                small_copy(2 * i + 1, d, send_blk.at[i, d], recv_blk.at[i, me]).start()

        recv_blk[i, me] = send_blk[i, me]
        await_all(small_recv.at[2 * i + 1], recv_blk.at[i])
        best = lax.fori_loop(0, shards, lambda d, m: jnp.maximum(m, recv_blk[i, d]), far_tgt)
        total = lax.fori_loop(
            0, shards, lambda d, t: t + jnp.exp2(recv_blk[i, d] - best), jnp.exp2(far_tgt - best)
        )
        lse = best + jnp.log2(total) - tgt_norm
        if i == ITERS - 1:
            v_ref[...] = OUT * lse
        else:
            b_own[i + 1] = -KEEP_TAU * lse - tgt_norm
            b_all[i + 1, me] = b_own[i + 1]
            spread_b(i + 1)
            await_all(small_recv.at[2 * i + 2], b_all.at[i + 1])

    u_ref[...] = u_acc[...].T[:src_count, :]

    own_to_sibling().wait_send()

    @pl.loop(0, units)
    def _(u):
        for forward in (True, False):
            ring_copy(u, forward).wait_send()
            sibling_copy(u, forward).wait_send()

    for phase in range(2 * ITERS):
        await_all(small_send.at[phase], recv_blk.at[0])


def per_device(src_points, tgt_points, g_init, far_src, far_tgt, cand_owner, cand_local):
    src_count, depth, points = src_points.shape
    tgt_count = tgt_points.shape[0]
    pairs = src_count * cand_owner.shape[1]
    shards = lax.axis_size("src")
    units = shards // 2 - 1
    capacity = max(2, min(src_count // 2, 2 * pairs // shards))
    early = shards * capacity <= pairs and units >= 3
    parts = pairs if early else 1
    f32 = jnp.float32
    scratch = [
        pltpu.VMEM(src_points.shape, jnp.bfloat16),
        pltpu.VMEM(g_init.shape, f32),
        pltpu.VMEM(far_src.shape, f32),
        pltpu.VMEM(far_tgt.shape, f32),
        pltpu.SMEM(cand_owner.shape, jnp.int32),
        pltpu.SMEM(cand_local.shape, jnp.int32),
        pltpu.SemaphoreType.DMA((7,)),
        pltpu.VMEM((shards, tgt_count, depth, points), jnp.bfloat16),
        pltpu.VMEM((pairs, points, points), f32),
        pltpu.VMEM((src_count, points, depth), jnp.bfloat16),
        pltpu.VMEM((src_count, points, 128), f32),
        pltpu.VMEM((src_count, points, 128), f32),
        pltpu.VMEM((src_count, points, 128), f32),
        pltpu.VMEM((points, 128), f32),
        pltpu.VMEM((pairs, 1, points), f32),
        pltpu.VMEM((ITERS, tgt_count, points), f32),
        pltpu.VMEM((ITERS, shards, tgt_count, points), f32),
        pltpu.VMEM((ITERS, shards, tgt_count, points), f32),
        pltpu.VMEM((ITERS, shards, tgt_count, points), f32),
        pltpu.SMEM((shards, src_count), jnp.int32),
        pltpu.SMEM((shards, src_count), jnp.int32),
    ]
    scratch += [pltpu.SMEM((shards, n), jnp.int32) for n in (src_count,) + 3 * (capacity,)]
    scratch += [pltpu.VMEM((points, 128), f32)] * 2
    scratch += [pltpu.VMEM((parts, points, 128), f32)] * 2
    scratch += [pltpu.VMEM(tgt_points.shape, jnp.bfloat16)]
    sems = [units] * 4 + [1 + 2 * units] * 2
    scratch += [pltpu.SemaphoreType.DMA((n,)) for n in sems]
    scratch += [pltpu.SemaphoreType.DMA((2 * ITERS,))] * 2
    vmem = pl.BlockSpec(memory_space=pltpu.VMEM)
    hbm = pl.BlockSpec(memory_space=pltpu.HBM)
    return pl.pallas_call(
        functools.partial(kernel, shards, capacity, early),
        out_shape=(
            jax.ShapeDtypeStruct((src_count, points), f32),
            jax.ShapeDtypeStruct((tgt_count, points), f32),
        ),
        in_specs=[hbm] * 7,
        out_specs=(vmem, vmem),
        scratch_shapes=scratch,
        compiler_params=pltpu.CompilerParams(
            collective_id=0, has_side_effects=True, vmem_limit_bytes=VMEM_BYTES
        ),
    )(src_points, tgt_points, g_init, far_src, far_tgt, cand_owner, cand_local)


def solution(mesh):
    return jax.shard_map(
        per_device,
        mesh=mesh,
        in_specs=(
            P(("groups", "src"), None, None),
            P(("groups", "src"), None, None),
            P(("groups", "src"), None),
            P(("groups", "src"), None),
            P(("groups", "src"), None),
            P(("groups", "src"), None),
            P(("groups", "src"), None),
        ),
        out_specs=(P(("groups", "src"), None), P(("groups", "src"), None)),
        check_vma=False,
    )
```
